512 devices in a mesh: gx: 4 (over y), gy: 4 (over z_hi, core), gz: 32 (over z_lo, x).
Axes of the slice: x: 4, y: 4, z: 16 (z_hi: 2, z_lo: 8; z = z_hi * 8 + z_lo), core: 2. Of those that a mesh axis runs over, the one named last changes fastest.
Arguments:
- density: float32 [256, 256, 256], P(('gx', 'gz'), 'gy'), may hold values from 0.5 to 2
- pheromone: float32 [256, 256, 256], P(('gx', 'gz'), 'gy'), may hold values from -6 to 6
Outputs:
- new_density: float32 [256, 256, 256], P(('gx', 'gz'), 'gy')
- new_pheromone: float32 [256, 256, 256], P(('gx', 'gz'), 'gy')
The draws below stay inside these ranges and needn't reach their ends.
All inputs are finite; a program needn't handle non-finite values.
Results may differ from the reference program's by a relative error of at most 0.0003.
Values sent between devices are 32-bit elements; how exact they have to be, the bound alone decides.
A program may use at most 64 MiB of HBM per device.

```python
import math
import jax
import jax.numpy as jnp

NX = 256
NY = 256
NZ = 256


def steps_of(own_key, shape, pieces, low, high):
    factor_of, own = 1.0, jax.random.fold_in(own_key, 6)
    for position, shards_of in pieces:
        draws = jnp.exp(jax.random.uniform(jax.random.fold_in(own, position), (shards_of,), jnp.float32, low / len(pieces), high / len(pieces)))
        factor_of = factor_of * jnp.repeat(draws, shape[position] // shards_of).reshape([-1 if axis == position else 1 for axis in range(len(shape))])
    return factor_of


def gaussian(key, shape, deviation, most, pieces=(), dtype=jnp.bfloat16):
    level = steps_of(key, shape, pieces, -0.22, 0.18) if pieces else 1.0
    entries = jax.random.normal(key, shape, jnp.float32) * deviation * level
    return jnp.minimum(jnp.maximum(entries, -most), most).astype(dtype)


def setup_inputs(seed: int = 0) -> dict:
    key_list = jax.random.split(jax.random.key(seed), 3)
    density = jnp.clip(jnp.exp(math.log(2.0) - 1.3862944 * jax.random.uniform(key_list[0], (NX, NY, NZ), jnp.float32) ** steps_of(key_list[0], (NX, NY, NZ), ((0, 128), (1, 4)), -0.2, 0.2)), 0.5, 2.0)
    pheromone = gaussian(key_list[1], (NX, NY, NZ), 1.0, 6.0, ((0, 128), (1, 4)), jnp.float32)
    return {"density": density, "pheromone": pheromone}


step_chemo = 1.0e-4
step_motile = 2.0e-4
step_diffuse = 2.0e-4
step_secrete = 0.5
step_decay = 0.1


def wave_numbers(count):
    index = jnp.arange(count)
    signed = jnp.where(index < count // 2, index, index - count)
    deriv = jnp.where(index == count // 2, 0, signed)
    return signed.astype(jnp.float32), deriv.astype(jnp.float32)


def reference(density, pheromone):
    signed_x, deriv_x = wave_numbers(NX)
    signed_y, deriv_y = wave_numbers(NY)
    signed_z, deriv_z = wave_numbers(NZ)
    signed_x, deriv_x = signed_x[:, None, None], deriv_x[:, None, None]
    signed_y, deriv_y = signed_y[None, :, None], deriv_y[None, :, None]
    signed_z, deriv_z = signed_z[None, None, :], deriv_z[None, None, :]
    ksquare = signed_x * signed_x + signed_y * signed_y + signed_z * signed_z
    density_hat = jnp.fft.fftn(density)
    pheromone_hat = jnp.fft.fftn(pheromone)
    divergence = jnp.zeros_like(density_hat)
    for deriv in (deriv_x, deriv_y, deriv_z):
        gradient = jnp.fft.ifftn(1j * deriv * pheromone_hat).real
        flux_hat = jnp.fft.fftn(density * gradient)
        divergence = divergence + 1j * deriv * flux_hat
    new_density_hat = (density_hat - step_chemo * divergence) / (1.0 + step_motile * ksquare)
    new_pheromone_hat = (pheromone_hat + step_secrete * density_hat) / (1.0 + step_diffuse * ksquare + step_decay)
    new_density = jnp.fft.ifftn(new_density_hat).real
    new_pheromone = jnp.fft.ifftn(new_pheromone_hat).real
    return new_density, new_pheromone
```

```python
import functools

import jax
import jax.numpy as jnp
import numpy as np
from jax import lax
from jax.experimental import pallas as pl
from jax.experimental.pallas import tpu as pltpu
from jax.sharding import PartitionSpec as P

MESH = pl.DeviceIdType.MESH

N = 256
step_chemo = 1.0e-4
step_motile = 2.0e-4
step_diffuse = 2.0e-4
step_secrete = 0.5
step_decay = 0.1

GROUP = 16
ROWS = 256
LANES = 128


def tables():
    index = np.arange(N)
    gap = (index[:, None] - index[None, :]) % N
    wave = np.arange(1, N // 2)
    row = -(2.0 / N) * np.sum(
        wave[:, None] * np.sin(2.0 * np.pi * ((wave[:, None] * index[None, :]) % N) / N), axis=0
    )
    deriv = row[gap]
    angle = 2.0 * np.pi * ((index[:, None] * index[None, :]) % N) / N
    hartley = (np.cos(angle) + np.sin(angle)) / np.sqrt(N)
    place = np.arange(N)
    x2, zl, yc, xc = place // 128, (place // 16) % 8, (place // 4) % 4, place % 4
    order_x = 2 * (yc * 32 + zl * 4 + xc) + x2
    order_y = ((place // 64) % 2) * 128 + (place // 128) * 64 + place % 64
    pick = lambda m, o: m[o][:, o]
    mats = (
        deriv, hartley,
        pick(deriv, order_x), pick(hartley, order_x),
        pick(deriv, order_y).T, pick(hartley, order_y),
    )
    half = np.minimum(index, N - index).astype(np.float64) ** 2
    return [np.asarray(m, np.float32) for m in mats], half[order_x], half[order_y]


def dot(a, b):
    return jnp.dot(a, b, precision=lax.Precision.HIGHEST, preferred_element_type=jnp.float32)


def block(ref, i):
    return ref.at[pl.ds(pl.multiple_of(i * GROUP, GROUP), GROUP), :]


def regroup(src, dst):
    for j in range(GROUP):
        dst[pl.ds(j * GROUP, GROUP), :] = src[pl.ds(j, GROUP, stride=GROUP), :]


def to_plane(m):
    a, b = m[:128], m[128:]
    low = lax.broadcasted_iota(jnp.int32, (128, 128), 1) < 64
    turn = lambda v: pltpu.roll(v, 64, 1)
    return jnp.concatenate([jnp.where(low, a, turn(b)), jnp.where(low, turn(a), b)], axis=0)


def kernel(
    dens_ref, pher_ref, dz, hz, dx, hx, dy, hy, mx_ref, my_ref,
    out_d, out_p,
    buf, full, base, filt, send_sem, recv_sem, core_send, core_recv,
):
    gx, gy, gz = lax.axis_index("gx"), lax.axis_index("gy"), lax.axis_index("gz")
    xc, yc, core = gz % 4, gx, gy % 2
    zc = (gy // 2) * 8 + gz // 4
    col = yc * 4 + xc

    def device(x, y, z, c):
        return (y, (z // 8) * 2 + c, (z % 8) * 4 + x)

    def peer(kind, i):
        if kind == "z":
            far = 8 - i // 2
            z = lax.rem(zc + 16 + jnp.where(i % 2 == 1, far, -far), 16)
            return z, device(xc, yc, z, core)
        y, x = (yc + i // 4) % 4, (xc + i % 4) % 4
        return y * 4 + x, device(x, y, zc, core)

    sibling = device(xc, yc, zc, 1 - core)
    barrier = pltpu.get_barrier_semaphore()
    for kind in ("z", "xy"):
        def greet(i, carry, kind=kind):
            pl.semaphore_signal(barrier, inc=1, device_id=peer(kind, i)[1], device_id_type=MESH)
            return carry
        lax.fori_loop(1, GROUP, greet, 0)
    pl.semaphore_signal(barrier, inc=1, device_id=sibling, device_id_type=MESH)

    def start(kind, src, dst, n):
        mine = zc if kind == "z" else col
        target = block(buf.at[dst], mine)
        def send(i, carry):
            number, where = peer(kind, i)
            pltpu.make_async_remote_copy(
                src_ref=block(buf.at[src], number), dst_ref=target,
                send_sem=send_sem.at[n], recv_sem=recv_sem.at[n],
                device_id=where, device_id_type=MESH,
            ).start()
            return carry
        lax.fori_loop(1, GROUP, send, 0)
        pltpu.make_async_copy(block(buf.at[src], mine), target, recv_sem.at[n]).start()

    def arrived(dst, n):
        pltpu.make_async_copy(buf.at[dst], buf.at[dst], recv_sem.at[n]).wait()

    FIRST = {"out": "xy", "back": "z"}
    SECOND = {"out": "z", "back": "xy"}

    def leave(trip, way, value):
        buf[4 * trip] = value
        start(FIRST[way], 4 * trip, 4 * trip + 1, 2 * trip)

    def forward(trip, way):
        arrived(4 * trip + 1, 2 * trip)
        regroup(buf.at[4 * trip + 1], buf.at[4 * trip + 2])
        start(SECOND[way], 4 * trip + 2, 4 * trip + 3, 2 * trip + 1)

    def land(trip):
        arrived(4 * trip + 3, 2 * trip + 1)
        return buf[4 * trip + 3]

    def share(k, value):
        full[k, core] = value
        pltpu.make_async_remote_copy(
            src_ref=full.at[k, core], dst_ref=full.at[k, core],
            send_sem=core_send.at[k], recv_sem=core_recv.at[k],
            device_id=sibling, device_id_type=MESH,
        ).start()

    def shared(k):
        other = full.at[k, 1 - core]
        pltpu.make_async_copy(other, other, core_recv.at[k]).wait()
        return jnp.concatenate([full[k, 0], full[k, 1]], axis=1)

    own = pl.ds(pl.multiple_of(core * LANES, LANES), LANES)
    RHO, CHEM, PLUS, TERM, PLUS_BACK, MOVED, MOVED_BACK = range(7)

    rho = dens_ref[...].T
    chem = pher_ref[...].T
    pl.semaphore_wait(barrier, 2 * (GROUP - 1) + 1)
    leave(RHO, "out", rho)
    leave(CHEM, "out", chem)
    leave(PLUS, "out", dot(hz[...], chem + step_secrete * rho))
    forward(RHO, "out")
    forward(CHEM, "out")
    base[...] = rho - step_chemo * dot(dz[...], rho * dot(dz[...], chem))
    forward(PLUS, "out")
    wave = (col * GROUP + zc).astype(jnp.float32)
    wave = jnp.minimum(wave, N - wave)
    ksquare = mx_ref[...] + my_ref[...] + wave * wave
    filt[0] = 1.0 / (1.0 + step_motile * ksquare)
    filt[1] = 1.0 / (1.0 + step_diffuse * ksquare + step_decay)

    rho_own = to_plane(land(RHO))
    share(0, rho_own)
    chem_own = to_plane(land(CHEM))
    share(1, chem_own)
    term = dot(dx[...], rho_own * dot(dx[...], chem_own))
    rho_all, chem_all = shared(0), shared(1)
    term = term + dot(rho_all * dot(chem_all, dy[...]), dy[:, own])
    leave(TERM, "back", to_plane(term))

    def solve(which, plane):
        modes = dot(dot(hx[...], plane), hy[...]) * filt[which]
        return to_plane(dot(hx[...], dot(modes, hy[:, own])))

    share(2, to_plane(land(PLUS)))
    forward(TERM, "back")
    leave(PLUS_BACK, "back", solve(1, shared(2)))
    moved = base[...] - step_chemo * land(TERM)
    leave(MOVED, "out", dot(hz[...], moved))
    forward(PLUS_BACK, "back")
    forward(MOVED, "out")
    out_p[...] = dot(hz[...], land(PLUS_BACK)).T
    share(3, to_plane(land(MOVED)))
    leave(MOVED_BACK, "back", solve(0, shared(3)))
    forward(MOVED_BACK, "back")
    out_d[...] = dot(hz[...], land(MOVED_BACK)).T

    def sent(n, carry):
        pltpu.make_async_copy(
            buf.at[0, pl.ds(0, ROWS - GROUP)], buf.at[0, pl.ds(0, ROWS - GROUP)], send_sem.at[n]
        ).wait()
        return carry
    lax.fori_loop(0, 14, sent, 0)
    def core_sent(k, carry):
        pltpu.make_async_copy(full.at[0, 0], full.at[0, 0], core_send.at[k]).wait()
        return carry
    lax.fori_loop(0, 4, core_sent, 0)


def per_device(density, pheromone):
    mats, mx, my = tables()
    mx = np.asarray(np.broadcast_to(mx[:, None], (N, N)), np.float32)
    my = np.asarray(np.broadcast_to(my[None, :], (8, N))[:1], np.float32)
    vmem = pl.BlockSpec(memory_space=pltpu.VMEM)
    flat = jax.ShapeDtypeStruct((LANES, N), jnp.float32)
    new_d, new_p = pl.pallas_call(
        kernel,
        out_shape=(flat, flat),
        in_specs=[vmem] * 10,
        out_specs=(vmem, vmem),
        scratch_shapes=[
            pltpu.VMEM((28, ROWS, LANES), jnp.float32),
            pltpu.VMEM((4, 2, N, LANES), jnp.float32),
            pltpu.VMEM((ROWS, LANES), jnp.float32),
            pltpu.VMEM((2, N, N), jnp.float32),
            pltpu.SemaphoreType.DMA((14,)),
            pltpu.SemaphoreType.DMA((14,)),
            pltpu.SemaphoreType.DMA((4,)),
            pltpu.SemaphoreType.DMA((4,)),
        ],
        compiler_params=pltpu.CompilerParams(
            collective_id=0, has_side_effects=True, vmem_limit_bytes=40 << 20
        ),
        name="chemotaxis_step",
    )(density.reshape(LANES, N), pheromone.reshape(LANES, N), *mats, mx, my)
    return new_d.reshape(density.shape), new_p.reshape(density.shape)


def solution(mesh):
    placed = (P(("gx", "gz"), "gy", None), P(("gx", "gz"), "gy", None))
    return jax.shard_map(
        per_device, mesh=mesh, in_specs=placed, out_specs=placed, check_vma=False
    )
```

```python
import functools

import jax
import jax.numpy as jnp
import numpy as np
from jax import lax
from jax.experimental import pallas as pl
from jax.experimental.pallas import tpu as pltpu
from jax.sharding import PartitionSpec as P

MESH = pl.DeviceIdType.MESH

N = 256
step_chemo = 1.0e-4
step_motile = 2.0e-4
step_diffuse = 2.0e-4
step_secrete = 0.5
step_decay = 0.1

GROUP = 16
ROWS = 256
LANES = 128


def tables():
    index = np.arange(N)
    gap = (index[:, None] - index[None, :]) % N
    wave = np.arange(1, N // 2)
    row = -(2.0 / N) * np.sum(
        wave[:, None] * np.sin(2.0 * np.pi * ((wave[:, None] * index[None, :]) % N) / N), axis=0
    )
    deriv = row[gap]
    angle = 2.0 * np.pi * ((index[:, None] * index[None, :]) % N) / N
    hartley = (np.cos(angle) + np.sin(angle)) / np.sqrt(N)
    place = np.arange(N)
    x2, zl, yc, xc = place // 128, (place // 16) % 8, (place // 4) % 4, place % 4
    order_x = 2 * (yc * 32 + zl * 4 + xc) + x2
    order_y = ((place // 64) % 2) * 128 + (place // 128) * 64 + place % 64
    pick = lambda m, o: m[o][:, o]
    mats = (
        deriv, hartley,
        pick(deriv, order_x), pick(hartley, order_x),
        pick(deriv, order_y).T, pick(hartley, order_y),
    )
    half = np.minimum(index, N - index).astype(np.float64) ** 2
    return [np.asarray(m, np.float32) for m in mats], half[order_x], half[order_y]


def dot(a, b):
    return jnp.dot(a, b, precision=lax.Precision.HIGHEST, preferred_element_type=jnp.float32)


def block(ref, i):
    return ref.at[pl.ds(pl.multiple_of(i * GROUP, GROUP), GROUP), :]


def regroup(src, dst):
    for j in range(GROUP):
        dst[pl.ds(j * GROUP, GROUP), :] = src[pl.ds(j, GROUP, stride=GROUP), :]


def to_plane(m):
    a, b = m[:128], m[128:]
    low = lax.broadcasted_iota(jnp.int32, (128, 128), 1) < 64
    turn = lambda v: pltpu.roll(v, 64, 1)
    return jnp.concatenate([jnp.where(low, a, turn(b)), jnp.where(low, turn(a), b)], axis=0)


def kernel(
    dens_ref, pher_ref, mats_ref, marks_ref,
    out_d, out_p,
    fields, mats, marks, buf, full, base, filt,
    load_sem, send_sem, recv_sem, core_send, core_recv,
):
    loads = [
        pltpu.make_async_copy(dens_ref, fields.at[0], load_sem.at[0]),
        pltpu.make_async_copy(pher_ref, fields.at[1], load_sem.at[1]),
        pltpu.make_async_copy(mats_ref, mats, load_sem.at[2]),
        pltpu.make_async_copy(marks_ref, marks, load_sem.at[3]),
    ]
    for load in loads:
        load.start()
    dz, hz, dx, hx, dy, hy = (mats.at[i] for i in range(6))
    gx, gy, gz = lax.axis_index("gx"), lax.axis_index("gy"), lax.axis_index("gz")
    xc, yc, core = gz % 4, gx, gy % 2
    zc = (gy // 2) * 8 + gz // 4
    col = yc * 4 + xc

    def device(x, y, z, c):
        return (y, (z // 8) * 2 + c, (z % 8) * 4 + x)

    def peer(kind, i):
        if kind == "z":
            far = 8 - i // 2
            z = lax.rem(zc + 16 + jnp.where(i % 2 == 1, far, -far), 16)
            return z, device(xc, yc, z, core)
        y, x = (yc + i // 4) % 4, (xc + i % 4) % 4
        return y * 4 + x, device(x, y, zc, core)

    sibling = device(xc, yc, zc, 1 - core)
    barrier = pltpu.get_barrier_semaphore()
    for kind in ("z", "xy"):
        def greet(i, carry, kind=kind):
            pl.semaphore_signal(barrier, inc=1, device_id=peer(kind, i)[1], device_id_type=MESH)
            return carry
        lax.fori_loop(1, GROUP, greet, 0)
    pl.semaphore_signal(barrier, inc=1, device_id=sibling, device_id_type=MESH)

    def start(kind, src, dst, n):
        mine = zc if kind == "z" else col
        target = block(buf.at[dst], mine)
        def send(i, carry):
            number, where = peer(kind, i)
            pltpu.make_async_remote_copy(
                src_ref=block(buf.at[src], number), dst_ref=target,
                send_sem=send_sem.at[n], recv_sem=recv_sem.at[n],
                device_id=where, device_id_type=MESH,
            ).start()
            return carry
        lax.fori_loop(1, GROUP, send, 0)
        pltpu.make_async_copy(block(buf.at[src], mine), target, recv_sem.at[n]).start()

    def arrived(dst, n):
        pltpu.make_async_copy(buf.at[dst], buf.at[dst], recv_sem.at[n]).wait()

    FIRST = {"out": "xy", "back": "z"}
    SECOND = {"out": "z", "back": "xy"}

    def leave(trip, way, value):
        buf[4 * trip] = value
        start(FIRST[way], 4 * trip, 4 * trip + 1, 2 * trip)

    def forward(trip, way):
        arrived(4 * trip + 1, 2 * trip)
        regroup(buf.at[4 * trip + 1], buf.at[4 * trip + 2])
        start(SECOND[way], 4 * trip + 2, 4 * trip + 3, 2 * trip + 1)

    def land(trip):
        arrived(4 * trip + 3, 2 * trip + 1)
        return buf[4 * trip + 3]

    def share(k, value):
        full[k, core] = value
        pltpu.make_async_remote_copy(
            src_ref=full.at[k, core], dst_ref=full.at[k, core],
            send_sem=core_send.at[k], recv_sem=core_recv.at[k],
            device_id=sibling, device_id_type=MESH,
        ).start()

    def shared(k):
        other = full.at[k, 1 - core]
        pltpu.make_async_copy(other, other, core_recv.at[k]).wait()
        return jnp.concatenate([full[k, 0], full[k, 1]], axis=1)

    own = pl.ds(pl.multiple_of(core * LANES, LANES), LANES)
    RHO, CHEM, PLUS, TERM, PLUS_BACK, MOVED, MOVED_BACK = range(7)

    loads[0].wait()
    rho = fields[0].T
    loads[1].wait()
    chem = fields[1].T
    pl.semaphore_wait(barrier, 2 * (GROUP - 1) + 1)
    leave(RHO, "out", rho)
    leave(CHEM, "out", chem)
    loads[2].wait()
    leave(PLUS, "out", dot(hz[...], chem + step_secrete * rho))
    forward(RHO, "out")
    forward(CHEM, "out")
    base[...] = rho - step_chemo * dot(dz[...], rho * dot(dz[...], chem))
    forward(PLUS, "out")
    wave = (col * GROUP + zc).astype(jnp.float32)
    wave = jnp.minimum(wave, N - wave)
    loads[3].wait()
    ksquare = marks[...] + wave * wave
    filt[0] = 1.0 / (1.0 + step_motile * ksquare)
    filt[1] = 1.0 / (1.0 + step_diffuse * ksquare + step_decay)

    rho_own = to_plane(land(RHO))
    share(0, rho_own)
    chem_own = to_plane(land(CHEM))
    share(1, chem_own)
    term = dot(dx[...], rho_own * dot(dx[...], chem_own))
    rho_all, chem_all = shared(0), shared(1)
    term = term + dot(rho_all * dot(chem_all, dy[...]), dy[:, own])
    leave(TERM, "back", to_plane(term))

    def solve(which, plane):
        modes = dot(dot(hx[...], plane), hy[...]) * filt[which]
        return to_plane(dot(hx[...], dot(modes, hy[:, own])))

    share(2, to_plane(land(PLUS)))
    forward(TERM, "back")
    leave(PLUS_BACK, "back", solve(1, shared(2)))
    moved = base[...] - step_chemo * land(TERM)
    leave(MOVED, "out", dot(hz[...], moved))
    forward(PLUS_BACK, "back")
    forward(MOVED, "out")
    out_p[...] = dot(hz[...], land(PLUS_BACK)).T
    share(3, to_plane(land(MOVED)))
    leave(MOVED_BACK, "back", solve(0, shared(3)))
    forward(MOVED_BACK, "back")
    out_d[...] = dot(hz[...], land(MOVED_BACK)).T

    def sent(n, carry):
        pltpu.make_async_copy(
            buf.at[0, pl.ds(0, ROWS - GROUP)], buf.at[0, pl.ds(0, ROWS - GROUP)], send_sem.at[n]
        ).wait()
        return carry
    lax.fori_loop(0, 14, sent, 0)
    def core_sent(k, carry):
        pltpu.make_async_copy(full.at[0, 0], full.at[0, 0], core_send.at[k]).wait()
        return carry
    lax.fori_loop(0, 4, core_sent, 0)


def per_device(density, pheromone):
    mats, mx, my = tables()
    marks = np.asarray(mx[:, None] + my[None, :], np.float32)
    hbm = pl.BlockSpec(memory_space=pltpu.HBM)
    vmem = pl.BlockSpec(memory_space=pltpu.VMEM)
    flat = jax.ShapeDtypeStruct((LANES, N), jnp.float32)
    new_d, new_p = pl.pallas_call(
        kernel,
        out_shape=(flat, flat),
        in_specs=[hbm] * 4,
        out_specs=(vmem, vmem),
        scratch_shapes=[
            pltpu.VMEM((2, LANES, N), jnp.float32),
            pltpu.VMEM((6, N, N), jnp.float32),
            pltpu.VMEM((N, N), jnp.float32),
            pltpu.VMEM((28, ROWS, LANES), jnp.float32),
            pltpu.VMEM((4, 2, N, LANES), jnp.float32),
            pltpu.VMEM((ROWS, LANES), jnp.float32),
            pltpu.VMEM((2, N, N), jnp.float32),
            pltpu.SemaphoreType.DMA((4,)),
            pltpu.SemaphoreType.DMA((14,)),
            pltpu.SemaphoreType.DMA((14,)),
            pltpu.SemaphoreType.DMA((4,)),
            pltpu.SemaphoreType.DMA((4,)),
        ],
        compiler_params=pltpu.CompilerParams(
            collective_id=0, has_side_effects=True, vmem_limit_bytes=60 << 20
        ),
        name="chemotaxis_step",
    )(density.reshape(LANES, N), pheromone.reshape(LANES, N), np.stack(mats), marks)
    return new_d.reshape(density.shape), new_p.reshape(density.shape)


def solution(mesh):
    placed = (P(("gx", "gz"), "gy", None), P(("gx", "gz"), "gy", None))
    return jax.shard_map(
        per_device, mesh=mesh, in_specs=placed, out_specs=placed, check_vma=False
    )
```

```python
import functools

import jax
import jax.numpy as jnp
import numpy as np
from jax import lax
from jax.experimental import pallas as pl
from jax.experimental.pallas import tpu as pltpu
from jax.sharding import PartitionSpec as P

MESH = pl.DeviceIdType.MESH

N = 256
step_chemo = 1.0e-4
step_motile = 2.0e-4
step_diffuse = 2.0e-4
step_secrete = 0.5
step_decay = 0.1

GROUP = 16
ROWS = 256
LANES = 128


def tables():
    index = np.arange(N)
    gap = (index[:, None] - index[None, :]) % N
    wave = np.arange(1, N // 2)
    row = -(2.0 / N) * np.sum(
        wave[:, None] * np.sin(2.0 * np.pi * ((wave[:, None] * index[None, :]) % N) / N), axis=0
    )
    deriv = row[gap]
    angle = 2.0 * np.pi * ((index[:, None] * index[None, :]) % N) / N
    hartley = (np.cos(angle) + np.sin(angle)) / np.sqrt(N)
    place = np.arange(N)
    x2, zl, yc, xc = place // 128, (place // 16) % 8, (place // 4) % 4, place % 4
    order_x = 2 * (yc * 32 + zl * 4 + xc) + x2
    order_y = ((place // 64) % 2) * 128 + (place // 128) * 64 + place % 64
    pick = lambda m, o: m[o][:, o]
    mats = (
        deriv, hartley,
        pick(deriv, order_x), pick(hartley, order_x),
        pick(deriv, order_y).T, pick(hartley, order_y),
    )
    half = np.minimum(index, N - index).astype(np.float64) ** 2
    return [np.asarray(m, np.float32) for m in mats], half[order_x], half[order_y]


def split(value):
    high = value.astype(jnp.bfloat16)
    return high, (value - high.astype(jnp.float32)).astype(jnp.bfloat16)


def dot(a, b):
    mul = functools.partial(jnp.dot, preferred_element_type=jnp.float32)
    return mul(a[0], b[0]) + (mul(a[0], b[1]) + mul(a[1], b[0]))


def row(ref, i):
    return ref.at[pl.ds(i, 1), :]


def to_plane(m):
    a, b = m[:128], m[128:]
    low = lax.broadcasted_iota(jnp.int32, (128, 128), 1) < 64
    turn = lambda v: pltpu.roll(v, 64, 1)
    return jnp.concatenate([jnp.where(low, a, turn(b)), jnp.where(low, turn(a), b)], axis=0)


def kernel(
    dens_ref, pher_ref, mats_ref, marks_ref,
    out_d, out_p,
    fields, exact, mats, marks, buf, full, base, filt,
    load_sem, send_sem, recv_sem, core_send, core_recv,
):
    loads = [
        pltpu.make_async_copy(dens_ref, fields.at[0], load_sem.at[0]),
        pltpu.make_async_copy(pher_ref, fields.at[1], load_sem.at[1]),
        pltpu.make_async_copy(mats_ref, exact, load_sem.at[2]),
        pltpu.make_async_copy(marks_ref, marks, load_sem.at[3]),
    ]
    for load in loads:
        load.start()
    dz, hz, dx, hx, dy, hy = range(6)

    def table(i):
        return mats[2 * i], mats[2 * i + 1]

    def left(i, value):
        return dot(table(i), split(value))

    def right(value, i):
        return dot(split(value), table(i))

    def right_own(value, i):
        return dot(split(value), (mats[2 * i, :, own], mats[2 * i + 1, :, own]))

    gx, gy, gz = lax.axis_index("gx"), lax.axis_index("gy"), lax.axis_index("gz")
    xc, yc, core = gz % 4, gx, gy % 2
    zc = (gy // 2) * 8 + gz // 4
    col = yc * 4 + xc
    own = pl.ds(pl.multiple_of(core * LANES, LANES), LANES)

    def device(x, y, z, c):
        return (y, (z // 8) * 2 + c, (z % 8) * 4 + x)

    def each_chip(act, mine):
        def some(i, carry):
            far = 8 - i // 4
            y = (yc + 2 + i) % 4
            ahead, behind = (zc + far) % 16, (zc + 17 - far) % 16
            for dx_ in (2, 1, 3, 0):
                x = (xc + dx_) % 4
                act(x, y, ahead)
                if dx_:
                    act(x, y, behind)
                else:
                    here = i == 30
                    pl.when(jnp.logical_not(here))(lambda: act(x, y, behind))
                    pl.when(here)(mine)
            return carry
        lax.fori_loop(0, 32, some, 0)

    sibling = device(xc, yc, zc, 1 - core)
    barrier = pltpu.get_barrier_semaphore()

    def greet(where):
        pl.semaphore_signal(barrier, inc=1, device_id=where, device_id_type=MESH)

    each_chip(lambda x, y, z: greet(device(x, y, z, core)), lambda: greet(sibling))

    def place(way, column, z):
        return column * GROUP + z if way == "out" else z * GROUP + column

    def leave(trip, way, value):
        src, dst = buf.at[2 * trip], buf.at[2 * trip + 1]
        buf[2 * trip] = value
        target = row(dst, zc * GROUP + col if way == "out" else col * GROUP + zc)

        def send(x, y, z):
            pltpu.make_async_remote_copy(
                src_ref=row(src, place(way, y * 4 + x, z)), dst_ref=target,
                send_sem=send_sem.at[trip], recv_sem=recv_sem.at[trip],
                device_id=device(x, y, z, core), device_id_type=MESH,
            ).start()

        def keep():
            pltpu.make_async_copy(row(src, place(way, col, zc)), target, recv_sem.at[trip]).start()

        each_chip(send, keep)

    def land(trip):
        dst = buf.at[2 * trip + 1]
        pltpu.make_async_copy(dst, dst, recv_sem.at[trip]).wait()
        return dst[...]

    def share(k, value):
        full[k, core] = value
        pltpu.make_async_remote_copy(
            src_ref=full.at[k, core], dst_ref=full.at[k, core],
            send_sem=core_send.at[k], recv_sem=core_recv.at[k],
            device_id=sibling, device_id_type=MESH,
        ).start()

    def shared(k):
        other = full.at[k, 1 - core]
        pltpu.make_async_copy(other, other, core_recv.at[k]).wait()
        return jnp.concatenate([full[k, 0], full[k, 1]], axis=1)

    RHO, CHEM, PLUS, TERM, PLUS_BACK, MOVED, MOVED_BACK = range(7)

    loads[0].wait()
    rho = fields[0].T
    loads[1].wait()
    chem = fields[1].T
    loads[2].wait()
    for i in range(6):
        mats[2 * i], mats[2 * i + 1] = split(exact[i])
    pl.semaphore_wait(barrier, ROWS)
    leave(RHO, "out", rho)
    leave(CHEM, "out", chem)
    leave(PLUS, "out", left(hz, chem + step_secrete * rho))
    base[...] = rho - step_chemo * left(dz, rho * left(dz, chem))
    wave = (col * GROUP + zc).astype(jnp.float32)
    wave = jnp.minimum(wave, N - wave)
    loads[3].wait()
    ksquare = marks[...] + wave * wave
    filt[0] = 1.0 / (1.0 + step_motile * ksquare)
    filt[1] = 1.0 / (1.0 + step_diffuse * ksquare + step_decay)

    rho_own = to_plane(land(RHO))
    share(0, rho_own)
    chem_own = to_plane(land(CHEM))
    share(1, chem_own)
    term = left(dx, rho_own * left(dx, chem_own))
    rho_all, chem_all = shared(0), shared(1)
    term = term + right_own(rho_all * right(chem_all, dy), dy)
    leave(TERM, "back", to_plane(term))

    def solve(which, plane):
        modes = right(left(hx, plane), hy) * filt[which]
        return to_plane(left(hx, right_own(modes, hy)))

    share(2, to_plane(land(PLUS)))
    plus = solve(1, shared(2))
    leave(MOVED, "out", left(hz, base[...] - step_chemo * land(TERM)))
    leave(PLUS_BACK, "back", plus)
    share(3, to_plane(land(MOVED)))
    leave(MOVED_BACK, "back", solve(0, shared(3)))
    out_p[...] = left(hz, land(PLUS_BACK)).T
    out_d[...] = left(hz, land(MOVED_BACK)).T

    def sent(n, carry):
        rest = buf.at[0, pl.ds(0, ROWS - 1), :]
        pltpu.make_async_copy(rest, rest, send_sem.at[n]).wait()
        return carry
    lax.fori_loop(0, 7, sent, 0)
    def core_sent(k, carry):
        pltpu.make_async_copy(full.at[0, 0], full.at[0, 0], core_send.at[k]).wait()
        return carry
    lax.fori_loop(0, 4, core_sent, 0)


def per_device(density, pheromone):
    mats, mx, my = tables()
    marks = np.asarray(mx[:, None] + my[None, :], np.float32)
    hbm = pl.BlockSpec(memory_space=pltpu.HBM)
    vmem = pl.BlockSpec(memory_space=pltpu.VMEM)
    flat = jax.ShapeDtypeStruct((LANES, N), jnp.float32)
    new_d, new_p = pl.pallas_call(
        kernel,
        out_shape=(flat, flat),
        in_specs=[hbm] * 4,
        out_specs=(vmem, vmem),
        scratch_shapes=[
            pltpu.VMEM((2, LANES, N), jnp.float32),
            pltpu.VMEM((6, N, N), jnp.float32),
            pltpu.VMEM((12, N, N), jnp.bfloat16),
            pltpu.VMEM((N, N), jnp.float32),
            pltpu.VMEM((14, ROWS, LANES), jnp.float32),
            pltpu.VMEM((4, 2, N, LANES), jnp.float32),
            pltpu.VMEM((ROWS, LANES), jnp.float32),
            pltpu.VMEM((2, N, N), jnp.float32),
            pltpu.SemaphoreType.DMA((4,)),
            pltpu.SemaphoreType.DMA((7,)),
            pltpu.SemaphoreType.DMA((7,)),
            pltpu.SemaphoreType.DMA((4,)),
            pltpu.SemaphoreType.DMA((4,)),
        ],
        compiler_params=pltpu.CompilerParams(
            collective_id=0, has_side_effects=True, vmem_limit_bytes=60 << 20
        ),
        name="chemotaxis_step",
    )(density.reshape(LANES, N), pheromone.reshape(LANES, N), np.stack(mats), marks)
    return new_d.reshape(density.shape), new_p.reshape(density.shape)


def solution(mesh):
    placed = (P(("gx", "gz"), "gy", None), P(("gx", "gz"), "gy", None))
    return jax.shard_map(
        per_device, mesh=mesh, in_specs=placed, out_specs=placed, check_vma=False
    )
```

```python
import functools

import jax
import jax.numpy as jnp
import numpy as np
from jax import lax
from jax.experimental import pallas as pl
from jax.experimental.pallas import tpu as pltpu
from jax.sharding import PartitionSpec as P

MESH = pl.DeviceIdType.MESH

N = 256
step_chemo = 1.0e-4
step_motile = 2.0e-4
step_diffuse = 2.0e-4
step_secrete = 0.5
step_decay = 0.1

GROUP = 16
ROWS = 256
LANES = 128


def tables():
    index = np.arange(N)
    gap = (index[:, None] - index[None, :]) % N
    wave = np.arange(1, N // 2)
    row = -(2.0 / N) * np.sum(
        wave[:, None] * np.sin(2.0 * np.pi * ((wave[:, None] * index[None, :]) % N) / N), axis=0
    )
    deriv = row[gap]
    angle = 2.0 * np.pi * ((index[:, None] * index[None, :]) % N) / N
    hartley = (np.cos(angle) + np.sin(angle)) / np.sqrt(N)
    place = np.arange(N)
    x2, zl, yc, xc = place // 128, (place // 16) % 8, (place // 4) % 4, place % 4
    order_x = 2 * (yc * 32 + zl * 4 + xc) + x2
    order_y = ((place // 64) % 2) * 128 + (place // 128) * 64 + place % 64
    pick = lambda m, o: m[o][:, o]
    mats = (
        deriv, hartley,
        pick(deriv, order_x), pick(hartley, order_x),
        pick(deriv, order_y).T, pick(hartley, order_y),
    )
    half = np.minimum(index, N - index).astype(np.float64) ** 2
    return [np.asarray(m, np.float32) for m in mats], half[order_x], half[order_y]


def split(value):
    high = value.astype(jnp.bfloat16)
    return high, (value - high.astype(jnp.float32)).astype(jnp.bfloat16)


def dot(a, b):
    mul = functools.partial(jnp.dot, preferred_element_type=jnp.float32)
    return mul(a[0], b[0]) + (mul(a[0], b[1]) + mul(a[1], b[0]))


def block(ref, i):
    return ref.at[pl.ds(pl.multiple_of(i * GROUP, GROUP), GROUP), :]


def row(ref, i):
    return ref.at[pl.ds(i, 1), :]


def to_plane(m):
    a, b = m[:128], m[128:]
    low = lax.broadcasted_iota(jnp.int32, (128, 128), 1) < 64
    turn = lambda v: pltpu.roll(v, 64, 1)
    return jnp.concatenate([jnp.where(low, a, turn(b)), jnp.where(low, turn(a), b)], axis=0)


def kernel(
    dens_ref, pher_ref, mats_ref, marks_ref,
    out,
    fields, exact, mats, marks, buf, mid, turned, final, full, base, filt,
    load_sem, store_sem, mid_send, mid_recv, send_sem, recv_sem, core_send, core_recv, ready,
):
    loads = [
        pltpu.make_async_copy(dens_ref, fields.at[0], load_sem.at[0]),
        pltpu.make_async_copy(pher_ref, fields.at[1], load_sem.at[1]),
        pltpu.make_async_copy(mats_ref, exact, load_sem.at[2]),
        pltpu.make_async_copy(marks_ref, marks, load_sem.at[3]),
    ]
    for load in loads:
        load.start()
    dz, hz, dx, hx, dy, hy = range(6)

    def table(i):
        return mats[2 * i], mats[2 * i + 1]

    def left(i, value):
        return dot(table(i), split(value))

    def right(value, i):
        return dot(split(value), table(i))

    def right_own(value, i):
        return dot(split(value), (mats[2 * i, :, own], mats[2 * i + 1, :, own]))

    gx, gy, gz = lax.axis_index("gx"), lax.axis_index("gy"), lax.axis_index("gz")
    xc, yc, core = gz % 4, gx, gy % 2
    zc = (gy // 2) * 8 + gz // 4
    col = yc * 4 + xc
    own = pl.ds(pl.multiple_of(core * LANES, LANES), LANES)

    def device(x, y, z, c):
        return (y, (z // 8) * 2 + c, (z % 8) * 4 + x)

    def each_chip(act, mine):
        def some(i, carry):
            far = 8 - i // 4
            y = (yc + 2 + i) % 4
            ahead, behind = (zc + far) % 16, (zc + 17 - far) % 16
            for dx_ in (2, 1, 3, 0):
                x = (xc + dx_) % 4
                act(x, y, ahead)
                if dx_:
                    act(x, y, behind)
                else:
                    here = i == 30
                    pl.when(jnp.logical_not(here))(lambda: act(x, y, behind))
                    pl.when(here)(mine)
            return carry
        lax.fori_loop(0, 32, some, 0)

    sibling = device(xc, yc, zc, 1 - core)
    barrier = pltpu.get_barrier_semaphore()

    def greet(where):
        pl.semaphore_signal(barrier, inc=1, device_id=where, device_id_type=MESH)

    def tell(sem, hops):
        for way in (hops, GROUP - hops):
            pl.semaphore_signal(
                sem, inc=1, device_id=device(xc, yc, (zc + way) % GROUP, core), device_id_type=MESH
            )

    for i in range(1, GROUP):
        greet(device((xc + i % 4) % 4, (yc + i // 4) % 4, zc, core))
    for hops in (4, 3, 2, 1):
        tell(barrier, hops)
    greet(sibling)

    def place(way, column, z):
        return column * GROUP + z if way == "out" else z * GROUP + column

    def leave(trip, way, value):
        src, dst = buf.at[2 * trip], buf.at[2 * trip + 1]
        buf[2 * trip] = value
        target = row(dst, zc * GROUP + col if way == "out" else col * GROUP + zc)

        def send(x, y, z):
            pltpu.make_async_remote_copy(
                src_ref=row(src, place(way, y * 4 + x, z)), dst_ref=target,
                send_sem=send_sem.at[trip], recv_sem=recv_sem.at[trip],
                device_id=device(x, y, z, core), device_id_type=MESH,
            ).start()

        def keep():
            pltpu.make_async_copy(row(src, place(way, col, zc)), target, recv_sem.at[trip]).start()

        each_chip(send, keep)

    def across(field):
        src, dst = buf.at[2 * field], mid.at[field]
        target = block(dst, col)
        for i in range(1, GROUP):
            y, x = (yc + i // 4) % 4, (xc + i % 4) % 4
            pltpu.make_async_remote_copy(
                src_ref=block(src, y * 4 + x), dst_ref=target,
                send_sem=mid_send.at[field], recv_sem=mid_recv.at[field],
                device_id=device(x, y, zc, core), device_id_type=MESH,
            ).start()
        pltpu.make_async_copy(block(src, col), target, mid_recv.at[field]).start()

    def along(field):
        pltpu.make_async_copy(mid.at[field], mid.at[field], mid_recv.at[field]).wait()
        src, dst = turned.at[field], buf.at[2 * field + 1]
        for z in range(GROUP):
            src[pl.ds(z * GROUP, GROUP), :] = mid[field, pl.ds(z, GROUP, stride=GROUP), :]
        target = block(dst, zc)
        for hops in (8, 9, 7, 10, 6, 11, 5, 12, 4, 13, 3, 14, 2, 15, 1):
            z = (zc + hops) % GROUP
            pltpu.make_async_remote_copy(
                src_ref=block(src, z), dst_ref=target,
                send_sem=send_sem.at[field], recv_sem=recv_sem.at[field],
                device_id=device(xc, yc, z, core), device_id_type=MESH,
            ).start()
        pltpu.make_async_copy(block(src, zc), target, recv_sem.at[field]).start()

    def land(trip):
        dst = buf.at[2 * trip + 1]
        pltpu.make_async_copy(dst, dst, recv_sem.at[trip]).wait()
        return dst

    def landed(trip):
        return land(trip)[...]

    def share(k, value):
        full[k, core] = value
        pltpu.make_async_remote_copy(
            src_ref=full.at[k, core], dst_ref=full.at[k, core],
            send_sem=core_send.at[k], recv_sem=core_recv.at[k],
            device_id=sibling, device_id_type=MESH,
        ).start()

    def shared(k):
        other = full.at[k, 1 - core]
        pltpu.make_async_copy(other, other, core_recv.at[k]).wait()
        return other[...]

    def joined(mine, other):
        first = core == 0
        return jnp.concatenate([jnp.where(first, mine, other), jnp.where(first, other, mine)], axis=1)

    CHEM, RHO, PLUS, TERM, PLUS_BACK, MOVED, MOVED_BACK = range(7)

    loads[0].wait()
    rho = fields[0].T
    loads[1].wait()
    chem = fields[1].T
    loads[2].wait()
    for i in range(6):
        mats[2 * i], mats[2 * i + 1] = split(exact[i])
    buf[2 * RHO] = rho
    buf[2 * CHEM] = chem
    pl.semaphore_wait(barrier, 24)
    for hops in (4, 3, 2, 1):
        tell(ready.at[0], hops)
    for field in (CHEM, RHO):
        across(field)
    pl.semaphore_wait(ready.at[0], 8)
    tell(ready.at[1], 4)
    for field in (CHEM, RHO):
        along(field)
    pl.semaphore_wait(ready.at[1], 2)
    plus = left(hz, chem + step_secrete * rho)
    base[...] = rho - step_chemo * left(dz, rho * left(dz, chem))
    wave = (col * GROUP + zc).astype(jnp.float32)
    wave = jnp.minimum(wave, N - wave)
    loads[3].wait()
    ksquare = marks[...] + wave * wave
    filt[0] = 1.0 / (1.0 + step_motile * ksquare)
    filt[1] = 1.0 / (1.0 + step_diffuse * ksquare + step_decay)

    chem_own = to_plane(landed(CHEM))
    share(0, chem_own)
    leave(PLUS, "out", plus)
    slope_x = left(dx, chem_own)
    chem_other = shared(0)
    slope_y = right(joined(chem_own, chem_other), dy)
    rho_own = to_plane(landed(RHO))
    share(1, rho_own)
    term = left(dx, rho_own * slope_x)
    rho_other = shared(1)
    term = term + right_own(joined(rho_own, rho_other) * slope_y, dy)
    leave(TERM, "back", to_plane(term))

    def solve(which, k, trip):
        mine = to_plane(landed(trip))
        share(k, mine)
        mine = left(hx, mine)
        other = left(hx, shared(k))
        modes = right(joined(mine, other), hy) * filt[which]
        return to_plane(left(hx, right_own(modes, hy)))

    plus = solve(1, 2, PLUS)
    leave(MOVED, "out", left(hz, base[...] - step_chemo * landed(TERM)))
    leave(PLUS_BACK, "back", plus)
    leave(MOVED_BACK, "back", solve(0, 3, MOVED))

    def store(i, trip):
        final[i] = left(hz, landed(trip)).T
        move = pltpu.make_async_copy(final.at[i], out.at[i], store_sem.at[i])
        move.start()
        return move

    stores = [store(1, PLUS_BACK), store(0, MOVED_BACK)]

    def sent(sem, count):
        rest = buf.at[0, pl.ds(0, count), :]
        pltpu.make_async_copy(rest, rest, sem).wait()

    for field in (CHEM, RHO):
        sent(mid_send.at[field], ROWS - GROUP)
        sent(send_sem.at[field], ROWS - GROUP)
    for trip in (PLUS, TERM, PLUS_BACK, MOVED, MOVED_BACK):
        sent(send_sem.at[trip], ROWS - 1)
    def core_sent(k, carry):
        pltpu.make_async_copy(full.at[0, 0], full.at[0, 0], core_send.at[k]).wait()
        return carry
    lax.fori_loop(0, 4, core_sent, 0)
    for store in stores:
        store.wait()


CHUNK = 32


def finish(both_ref, dens_ref, pher_ref, held, in_sem, out_sem):
    parts = [(i, k) for i in range(2) for k in range(LANES // CHUNK)]

    def load(n, i, k):
        rows = pl.ds(k * CHUNK, CHUNK)
        return pltpu.make_async_copy(both_ref.at[i, rows, :], held.at[i, rows, :], in_sem.at[n])

    def store(n, i, k):
        rows = pl.ds(k * CHUNK, CHUNK)
        target = (dens_ref, pher_ref)[i]
        return pltpu.make_async_copy(held.at[i, rows, :], target.at[rows, :], out_sem.at[n])

    for n, (i, k) in enumerate(parts):
        load(n, i, k).start()
    for n, (i, k) in enumerate(parts):
        load(n, i, k).wait()
        store(n, i, k).start()
    for n, (i, k) in enumerate(parts):
        store(n, i, k).wait()


def per_device(density, pheromone):
    mats, mx, my = tables()
    marks = np.asarray(mx[:, None] + my[None, :], np.float32)
    hbm = pl.BlockSpec(memory_space=pltpu.HBM)
    flat = jax.ShapeDtypeStruct((LANES, N), jnp.float32)
    mats = np.stack(mats)
    both = pl.pallas_call(
        kernel,
        out_shape=jax.ShapeDtypeStruct((2, LANES, N), jnp.float32),
        in_specs=[hbm] * 4,
        out_specs=hbm,
        scratch_shapes=[
            pltpu.VMEM((2, LANES, N), jnp.float32),
            pltpu.VMEM((6, N, N), jnp.float32),
            pltpu.VMEM((12, N, N), jnp.bfloat16),
            pltpu.VMEM((N, N), jnp.float32),
            pltpu.VMEM((14, ROWS, LANES), jnp.float32),
            pltpu.VMEM((2, ROWS, LANES), jnp.float32),
            pltpu.VMEM((2, ROWS, LANES), jnp.float32),
            pltpu.VMEM((2, LANES, N), jnp.float32),
            pltpu.VMEM((4, 2, N, LANES), jnp.float32),
            pltpu.VMEM((ROWS, LANES), jnp.float32),
            pltpu.VMEM((2, N, N), jnp.float32),
            pltpu.SemaphoreType.DMA((4,)),
            pltpu.SemaphoreType.DMA((2,)),
            pltpu.SemaphoreType.DMA((2,)),
            pltpu.SemaphoreType.DMA((2,)),
            pltpu.SemaphoreType.DMA((7,)),
            pltpu.SemaphoreType.DMA((7,)),
            pltpu.SemaphoreType.DMA((4,)),
            pltpu.SemaphoreType.DMA((4,)),
            pltpu.SemaphoreType.REGULAR((2,)),
        ],
        compiler_params=pltpu.CompilerParams(
            collective_id=0, has_side_effects=True, vmem_limit_bytes=60 << 20
        ),
        name="chemotaxis_step",
    )(density.reshape(LANES, N), pheromone.reshape(LANES, N), mats, marks)
    flat = jax.ShapeDtypeStruct((LANES, N), jnp.float32)
    new_d, new_p = pl.pallas_call(
        finish,
        out_shape=(flat, flat),
        in_specs=[hbm],
        out_specs=(hbm, hbm),
        scratch_shapes=[
            pltpu.VMEM((2, LANES, N), jnp.float32),
            pltpu.SemaphoreType.DMA((2 * LANES // CHUNK,)),
            pltpu.SemaphoreType.DMA((2 * LANES // CHUNK,)),
        ],
        compiler_params=pltpu.CompilerParams(vmem_limit_bytes=60 << 20),
        name="outputs",
    )(both)
    return new_d.reshape(density.shape), new_p.reshape(density.shape)


def solution(mesh):
    placed = (P(("gx", "gz"), "gy", None), P(("gx", "gz"), "gy", None))
    return jax.shard_map(
        per_device, mesh=mesh, in_specs=placed, out_specs=placed, check_vma=False
    )
```

```python
import functools

import jax
import jax.numpy as jnp
import numpy as np
from jax import lax
from jax.experimental import pallas as pl
from jax.experimental.pallas import tpu as pltpu
from jax.sharding import PartitionSpec as P

MESH = pl.DeviceIdType.MESH

N = 256
step_chemo = 1.0e-4
step_motile = 2.0e-4
step_diffuse = 2.0e-4
step_secrete = 0.5
step_decay = 0.1

GROUP = 16
ROWS = 256
LANES = 128


def tables():
    index = np.arange(N)
    gap = (index[:, None] - index[None, :]) % N
    wave = np.arange(1, N // 2)
    row = -(2.0 / N) * np.sum(
        wave[:, None] * np.sin(2.0 * np.pi * ((wave[:, None] * index[None, :]) % N) / N), axis=0
    )
    deriv = row[gap]
    angle = 2.0 * np.pi * ((index[:, None] * index[None, :]) % N) / N
    hartley = (np.cos(angle) + np.sin(angle)) / np.sqrt(N)
    place = np.arange(N)
    x2, zl, yc, xc = place // 128, (place // 16) % 8, (place // 4) % 4, place % 4
    order_x = 2 * (yc * 32 + zl * 4 + xc) + x2
    order_y = ((place // 64) % 2) * 128 + (place // 128) * 64 + place % 64
    pick = lambda m, o: m[o][:, o]
    mats = (
        deriv, hartley,
        pick(deriv, order_x), pick(hartley, order_x),
        pick(deriv, order_y).T, pick(hartley, order_y),
    )
    half = np.minimum(index, N - index).astype(np.float64) ** 2
    return [np.asarray(m, np.float32) for m in mats], half[order_x], half[order_y]


def split(value):
    high = value.astype(jnp.bfloat16)
    return high, (value - high.astype(jnp.float32)).astype(jnp.bfloat16)


def dot(a, b):
    mul = functools.partial(jnp.dot, preferred_element_type=jnp.float32)
    return mul(a[0], b[0]) + (mul(a[0], b[1]) + mul(a[1], b[0]))


def block(ref, i):
    return ref.at[pl.ds(pl.multiple_of(i * GROUP, GROUP), GROUP), :]


def row(ref, i):
    return ref.at[pl.ds(i, 1), :]


def to_plane(m):
    a, b = m[:128], m[128:]
    low = lax.broadcasted_iota(jnp.int32, (128, 128), 1) < 64
    turn = lambda v: pltpu.roll(v, 64, 1)
    return jnp.concatenate([jnp.where(low, a, turn(b)), jnp.where(low, turn(a), b)], axis=0)


def kernel(
    dens_ref, pher_ref, mats_ref, marks_ref,
    out,
    fields, exact, mats, marks, buf, mid, turned, final, full, base, filt,
    load_sem, store_sem, mid_send, mid_recv, send_sem, recv_sem, core_send, core_recv, ready,
):
    loads = [
        pltpu.make_async_copy(dens_ref, fields.at[0], load_sem.at[0]),
        pltpu.make_async_copy(pher_ref, fields.at[1], load_sem.at[1]),
        pltpu.make_async_copy(mats_ref, exact, load_sem.at[2]),
        pltpu.make_async_copy(marks_ref, marks, load_sem.at[3]),
    ]
    for load in loads:
        load.start()
    dz, hz, dx, hx, dy, hy = range(6)

    def table(i):
        return mats[2 * i], mats[2 * i + 1]

    def left(i, value):
        return dot(table(i), split(value))

    def right(value, i):
        return dot(split(value), table(i))

    def right_own(value, i):
        return dot(split(value), (mats[2 * i, :, own], mats[2 * i + 1, :, own]))

    gx, gy, gz = lax.axis_index("gx"), lax.axis_index("gy"), lax.axis_index("gz")
    xc, yc, core = gz % 4, gx, gy % 2
    zc = (gy // 2) * 8 + gz // 4
    col = yc * 4 + xc
    own = pl.ds(pl.multiple_of(core * LANES, LANES), LANES)

    def device(x, y, z, c):
        return (y, (z // 8) * 2 + c, (z % 8) * 4 + x)

    def each_chip(act, mine):
        def some(i, carry):
            far = 8 - i // 4
            y = (yc + 2 + i) % 4
            ahead, behind = (zc + far) % 16, (zc + 17 - far) % 16
            for dx_ in (2, 1, 3, 0):
                x = (xc + dx_) % 4
                act(x, y, ahead)
                if dx_:
                    act(x, y, behind)
                else:
                    here = i == 30
                    pl.when(jnp.logical_not(here))(lambda: act(x, y, behind))
                    pl.when(here)(mine)
            return carry
        lax.fori_loop(0, 32, some, 0)

    sibling = device(xc, yc, zc, 1 - core)
    barrier = pltpu.get_barrier_semaphore()

    def greet(where):
        pl.semaphore_signal(barrier, inc=1, device_id=where, device_id_type=MESH)

    def tell(sem, hops):
        for way in (hops, GROUP - hops):
            pl.semaphore_signal(
                sem, inc=1, device_id=device(xc, yc, (zc + way) % GROUP, core), device_id_type=MESH
            )

    for i in range(1, GROUP):
        greet(device((xc + i % 4) % 4, (yc + i // 4) % 4, zc, core))
    for hops in (4, 3, 2, 1):
        tell(barrier, hops)
    greet(sibling)

    def place(way, column, z):
        return column * GROUP + z if way == "out" else z * GROUP + column

    def leave(trip, way, value):
        src, dst = buf.at[2 * trip], buf.at[2 * trip + 1]
        buf[2 * trip] = value
        target = row(dst, zc * GROUP + col if way == "out" else col * GROUP + zc)

        def send(x, y, z):
            pltpu.make_async_remote_copy(
                src_ref=row(src, place(way, y * 4 + x, z)), dst_ref=target,
                send_sem=send_sem.at[trip], recv_sem=recv_sem.at[trip],
                device_id=device(x, y, z, core), device_id_type=MESH,
            ).start()

        def keep():
            pltpu.make_async_copy(row(src, place(way, col, zc)), target, recv_sem.at[trip]).start()

        each_chip(send, keep)

    def across(field):
        src, dst = buf.at[2 * field], mid.at[field]
        target = block(dst, col)
        for i in range(1, GROUP):
            y, x = (yc + i // 4) % 4, (xc + i % 4) % 4
            pltpu.make_async_remote_copy(
                src_ref=block(src, y * 4 + x), dst_ref=target,
                send_sem=mid_send.at[field], recv_sem=mid_recv.at[field],
                device_id=device(x, y, zc, core), device_id_type=MESH,
            ).start()
        pltpu.make_async_copy(block(src, col), target, mid_recv.at[field]).start()

    def along(field):
        pltpu.make_async_copy(mid.at[field], mid.at[field], mid_recv.at[field]).wait()
        src, dst = turned.at[field], buf.at[2 * field + 1]
        for z in range(GROUP):
            src[pl.ds(z * GROUP, GROUP), :] = mid[field, pl.ds(z, GROUP, stride=GROUP), :]
        target = block(dst, zc)
        for hops in (8, 9, 7, 10, 6, 11, 5, 12, 4, 13, 3, 14, 2, 15, 1):
            z = (zc + hops) % GROUP
            pltpu.make_async_remote_copy(
                src_ref=block(src, z), dst_ref=target,
                send_sem=send_sem.at[field], recv_sem=recv_sem.at[field],
                device_id=device(xc, yc, z, core), device_id_type=MESH,
            ).start()
        pltpu.make_async_copy(block(src, zc), target, recv_sem.at[field]).start()

    def land(trip):
        dst = buf.at[2 * trip + 1]
        pltpu.make_async_copy(dst, dst, recv_sem.at[trip]).wait()
        return dst

    def landed(trip):
        return land(trip)[...]

    def share(k, value):
        full[k, core] = value
        pltpu.make_async_remote_copy(
            src_ref=full.at[k, core], dst_ref=full.at[k, core],
            send_sem=core_send.at[k], recv_sem=core_recv.at[k],
            device_id=sibling, device_id_type=MESH,
        ).start()

    def shared(k):
        other = full.at[k, 1 - core]
        pltpu.make_async_copy(other, other, core_recv.at[k]).wait()
        return other[...]

    def joined(mine, other):
        first = core == 0
        return jnp.concatenate([jnp.where(first, mine, other), jnp.where(first, other, mine)], axis=1)

    CHEM, RHO, PLUS, TERM, PLUS_BACK, MOVED, MOVED_BACK = range(7)

    loads[0].wait()
    rho = fields[0].T
    loads[1].wait()
    chem = fields[1].T
    loads[2].wait()
    for i in range(6):
        mats[2 * i], mats[2 * i + 1] = split(exact[i])
    buf[2 * RHO] = rho
    buf[2 * CHEM] = chem
    pl.semaphore_wait(barrier, 24)
    for hops in (4, 3, 2, 1):
        tell(ready.at[0], hops)
    for field in (CHEM, RHO):
        across(field)
    pl.semaphore_wait(ready.at[0], 8)
    tell(ready.at[1], 4)
    for field in (CHEM, RHO):
        along(field)
    pl.semaphore_wait(ready.at[1], 2)
    plus = left(hz, chem + step_secrete * rho)
    base[...] = rho - step_chemo * left(dz, rho * left(dz, chem))
    wave = (col * GROUP + zc).astype(jnp.float32)
    wave = jnp.minimum(wave, N - wave)
    loads[3].wait()
    ksquare = marks[...] + wave * wave
    filt[0] = 1.0 / (1.0 + step_motile * ksquare)
    filt[1] = 1.0 / (1.0 + step_diffuse * ksquare + step_decay)

    chem_own = to_plane(landed(CHEM))
    share(0, chem_own)
    slope_x = left(dx, chem_own)
    chem_other = shared(0)
    slope_y = right(joined(chem_own, chem_other), dy)
    rho_own = to_plane(landed(RHO))
    share(1, rho_own)
    term = left(dx, rho_own * slope_x)
    rho_other = shared(1)
    term = term + right_own(joined(rho_own, rho_other) * slope_y, dy)
    leave(TERM, "back", to_plane(term))
    leave(PLUS, "out", plus)

    def solve(which, k, trip):
        mine = to_plane(landed(trip))
        share(k, mine)
        mine = left(hx, mine)
        other = left(hx, shared(k))
        modes = right(joined(mine, other), hy) * filt[which]
        return to_plane(left(hx, right_own(modes, hy)))

    leave(MOVED, "out", left(hz, base[...] - step_chemo * landed(TERM)))
    leave(PLUS_BACK, "back", solve(1, 2, PLUS))
    leave(MOVED_BACK, "back", solve(0, 3, MOVED))

    def store(i, trip):
        final[i] = left(hz, landed(trip)).T
        move = pltpu.make_async_copy(final.at[i], out.at[i], store_sem.at[i])
        move.start()
        return move

    stores = [store(1, PLUS_BACK), store(0, MOVED_BACK)]

    def sent(sem, count):
        rest = buf.at[0, pl.ds(0, count), :]
        pltpu.make_async_copy(rest, rest, sem).wait()

    for field in (CHEM, RHO):
        sent(mid_send.at[field], ROWS - GROUP)
        sent(send_sem.at[field], ROWS - GROUP)
    for trip in (PLUS, TERM, PLUS_BACK, MOVED, MOVED_BACK):
        sent(send_sem.at[trip], ROWS - 1)
    def core_sent(k, carry):
        pltpu.make_async_copy(full.at[0, 0], full.at[0, 0], core_send.at[k]).wait()
        return carry
    lax.fori_loop(0, 4, core_sent, 0)
    for store in stores:
        store.wait()


CHUNK = 32


def finish(both_ref, dens_ref, pher_ref, held, in_sem, out_sem):
    parts = [(i, k) for i in range(2) for k in range(LANES // CHUNK)]

    def load(n, i, k):
        rows = pl.ds(k * CHUNK, CHUNK)
        return pltpu.make_async_copy(both_ref.at[i, rows, :], held.at[i, rows, :], in_sem.at[n])

    def store(n, i, k):
        rows = pl.ds(k * CHUNK, CHUNK)
        target = (dens_ref, pher_ref)[i]
        return pltpu.make_async_copy(held.at[i, rows, :], target.at[rows, :], out_sem.at[n])

    for n, (i, k) in enumerate(parts):
        load(n, i, k).start()
    for n, (i, k) in enumerate(parts):
        load(n, i, k).wait()
        store(n, i, k).start()
    for n, (i, k) in enumerate(parts):
        store(n, i, k).wait()


def per_device(density, pheromone):
    mats, mx, my = tables()
    marks = np.asarray(mx[:, None] + my[None, :], np.float32)
    hbm = pl.BlockSpec(memory_space=pltpu.HBM)
    flat = jax.ShapeDtypeStruct((LANES, N), jnp.float32)
    mats = np.stack(mats)
    both = pl.pallas_call(
        kernel,
        out_shape=jax.ShapeDtypeStruct((2, LANES, N), jnp.float32),
        in_specs=[hbm] * 4,
        out_specs=hbm,
        scratch_shapes=[
            pltpu.VMEM((2, LANES, N), jnp.float32),
            pltpu.VMEM((6, N, N), jnp.float32),
            pltpu.VMEM((12, N, N), jnp.bfloat16),
            pltpu.VMEM((N, N), jnp.float32),
            pltpu.VMEM((14, ROWS, LANES), jnp.float32),
            pltpu.VMEM((2, ROWS, LANES), jnp.float32),
            pltpu.VMEM((2, ROWS, LANES), jnp.float32),
            pltpu.VMEM((2, LANES, N), jnp.float32),
            pltpu.VMEM((4, 2, N, LANES), jnp.float32),
            pltpu.VMEM((ROWS, LANES), jnp.float32),
            pltpu.VMEM((2, N, N), jnp.float32),
            pltpu.SemaphoreType.DMA((4,)),
            pltpu.SemaphoreType.DMA((2,)),
            pltpu.SemaphoreType.DMA((2,)),
            pltpu.SemaphoreType.DMA((2,)),
            pltpu.SemaphoreType.DMA((7,)),
            pltpu.SemaphoreType.DMA((7,)),
            pltpu.SemaphoreType.DMA((4,)),
            pltpu.SemaphoreType.DMA((4,)),
            pltpu.SemaphoreType.REGULAR((2,)),
        ],
        compiler_params=pltpu.CompilerParams(
            collective_id=0, has_side_effects=True, vmem_limit_bytes=60 << 20
        ),
        name="chemotaxis_step",
    )(density.reshape(LANES, N), pheromone.reshape(LANES, N), mats, marks)
    flat = jax.ShapeDtypeStruct((LANES, N), jnp.float32)
    new_d, new_p = pl.pallas_call(
        finish,
        out_shape=(flat, flat),
        in_specs=[hbm],
        out_specs=(hbm, hbm),
        scratch_shapes=[
            pltpu.VMEM((2, LANES, N), jnp.float32),
            pltpu.SemaphoreType.DMA((2 * LANES // CHUNK,)),
            pltpu.SemaphoreType.DMA((2 * LANES // CHUNK,)),
        ],
        compiler_params=pltpu.CompilerParams(vmem_limit_bytes=60 << 20),
        name="outputs",
    )(both)
    return new_d.reshape(density.shape), new_p.reshape(density.shape)


def solution(mesh):
    placed = (P(("gx", "gz"), "gy", None), P(("gx", "gz"), "gy", None))
    return jax.shard_map(
        per_device, mesh=mesh, in_specs=placed, out_specs=placed, check_vma=False
    )
```

```python
import functools

import jax
import jax.numpy as jnp
import numpy as np
from jax import lax
from jax.experimental import pallas as pl
from jax.experimental.pallas import tpu as pltpu
from jax.sharding import PartitionSpec as P

MESH = pl.DeviceIdType.MESH

N = 256
step_chemo = 1.0e-4
step_motile = 2.0e-4
step_diffuse = 2.0e-4
step_secrete = 0.5
step_decay = 0.1

GROUP = 16
ROWS = 256
LANES = 128


def tables():
    index = np.arange(N)
    gap = (index[:, None] - index[None, :]) % N
    wave = np.arange(1, N // 2)
    row = -(2.0 / N) * np.sum(
        wave[:, None] * np.sin(2.0 * np.pi * ((wave[:, None] * index[None, :]) % N) / N), axis=0
    )
    deriv = row[gap]
    angle = 2.0 * np.pi * ((index[:, None] * index[None, :]) % N) / N
    hartley = (np.cos(angle) + np.sin(angle)) / np.sqrt(N)
    place = np.arange(N)
    x2, zl, yc, xc = place // 128, (place // 16) % 8, (place // 4) % 4, place % 4
    order_x = 2 * (yc * 32 + zl * 4 + xc) + x2
    order_y = ((place // 64) % 2) * 128 + (place // 128) * 64 + place % 64
    pick = lambda m, o: m[o][:, o]
    mats = (
        deriv, hartley,
        pick(deriv, order_x), pick(hartley, order_x),
        pick(deriv, order_y).T, pick(hartley, order_y),
    )
    half = np.minimum(index, N - index).astype(np.float64) ** 2
    return [np.asarray(m, np.float32) for m in mats], half[order_x], half[order_y]


def split(value):
    high = value.astype(jnp.bfloat16)
    return high, (value - high.astype(jnp.float32)).astype(jnp.bfloat16)


def dot(a, b):
    mul = functools.partial(jnp.dot, preferred_element_type=jnp.float32)
    return mul(a[0], b[0]) + (mul(a[0], b[1]) + mul(a[1], b[0]))


def block(ref, i):
    return ref.at[pl.ds(pl.multiple_of(i * GROUP, GROUP), GROUP), :]


def row(ref, i):
    return ref.at[pl.ds(i, 1), :]


def to_plane(m):
    a, b = m[:128], m[128:]
    low = lax.broadcasted_iota(jnp.int32, (128, 128), 1) < 64
    turn = lambda v: pltpu.roll(v, 64, 1)
    return jnp.concatenate([jnp.where(low, a, turn(b)), jnp.where(low, turn(a), b)], axis=0)


def kernel(
    dens_ref, pher_ref, mats_ref, marks_ref,
    out,
    fields, exact, mats, marks, buf, mid, turned, final, full, base, filt,
    load_sem, store_sem, mid_send, mid_recv, send_sem, recv_sem, core_send, core_recv, ready,
):
    loads = [
        pltpu.make_async_copy(dens_ref, fields.at[0], load_sem.at[0]),
        pltpu.make_async_copy(pher_ref, fields.at[1], load_sem.at[1]),
        pltpu.make_async_copy(mats_ref, exact, load_sem.at[2]),
        pltpu.make_async_copy(marks_ref, marks, load_sem.at[3]),
    ]
    for load in loads:
        load.start()
    dz, hz, dx, hx, dy, hy = range(6)

    def table(i):
        return mats[2 * i], mats[2 * i + 1]

    def left(i, value):
        return dot(table(i), split(value))

    def right(value, i):
        return dot(split(value), table(i))

    def right_own(value, i):
        return dot(split(value), (mats[2 * i, :, own], mats[2 * i + 1, :, own]))

    gx, gy, gz = lax.axis_index("gx"), lax.axis_index("gy"), lax.axis_index("gz")
    xc, yc, core = gz % 4, gx, gy % 2
    zc = (gy // 2) * 8 + gz // 4
    col = yc * 4 + xc
    own = pl.ds(pl.multiple_of(core * LANES, LANES), LANES)

    def device(x, y, z, c):
        return (y, (z // 8) * 2 + c, (z % 8) * 4 + x)

    def each_chip(act, mine):
        def some(i, carry):
            far = 8 - i // 4
            y = (yc + 2 + i) % 4
            ahead, behind = (zc + far) % 16, (zc + 17 - far) % 16
            for dx_ in (2, 1, 3, 0):
                x = (xc + dx_) % 4
                act(x, y, ahead)
                if dx_:
                    act(x, y, behind)
                else:
                    here = i == 30
                    pl.when(jnp.logical_not(here))(lambda: act(x, y, behind))
                    pl.when(here)(mine)
            return carry
        lax.fori_loop(0, 32, some, 0)

    sibling = device(xc, yc, zc, 1 - core)
    barrier = pltpu.get_barrier_semaphore()

    def greet(where):
        pl.semaphore_signal(barrier, inc=1, device_id=where, device_id_type=MESH)

    def tell(sem, hops):
        for way in (hops, GROUP - hops):
            pl.semaphore_signal(
                sem, inc=1, device_id=device(xc, yc, (zc + way) % GROUP, core), device_id_type=MESH
            )

    tell(barrier, 4)
    for i in (10, 9, 11, 6, 14, 8, 2, 5, 7, 13, 15, 4, 12, 1, 3):
        greet(device((xc + i % 4) % 4, (yc + i // 4) % 4, zc, core))
    for hops in (3, 2, 1):
        tell(barrier, hops)
    greet(sibling)

    def place(way, column, z):
        return column * GROUP + z if way == "out" else z * GROUP + column

    def leave(trip, way, value):
        src, dst = buf.at[2 * trip], buf.at[2 * trip + 1]
        buf[2 * trip] = value
        target = row(dst, zc * GROUP + col if way == "out" else col * GROUP + zc)

        def send(x, y, z):
            pltpu.make_async_remote_copy(
                src_ref=row(src, place(way, y * 4 + x, z)), dst_ref=target,
                send_sem=send_sem.at[trip], recv_sem=recv_sem.at[trip],
                device_id=device(x, y, z, core), device_id_type=MESH,
            ).start()

        def keep():
            pltpu.make_async_copy(row(src, place(way, col, zc)), target, recv_sem.at[trip]).start()

        each_chip(send, keep)

    def across(field):
        src, dst = buf.at[2 * field], mid.at[field]
        target = block(dst, col)
        for i in range(1, GROUP):
            y, x = (yc + i // 4) % 4, (xc + i % 4) % 4
            pltpu.make_async_remote_copy(
                src_ref=block(src, y * 4 + x), dst_ref=target,
                send_sem=mid_send.at[field], recv_sem=mid_recv.at[field],
                device_id=device(x, y, zc, core), device_id_type=MESH,
            ).start()
        pltpu.make_async_copy(block(src, col), target, mid_recv.at[field]).start()

    def along(field):
        pltpu.make_async_copy(mid.at[field], mid.at[field], mid_recv.at[field]).wait()
        src, dst = turned.at[field], buf.at[2 * field + 1]
        for z in range(GROUP):
            src[pl.ds(z * GROUP, GROUP), :] = mid[field, pl.ds(z, GROUP, stride=GROUP), :]
        target = block(dst, zc)
        for hops in (8, 9, 7, 10, 6, 11, 5, 12, 4, 13, 3, 14, 2, 15, 1):
            z = (zc + hops) % GROUP
            pltpu.make_async_remote_copy(
                src_ref=block(src, z), dst_ref=target,
                send_sem=send_sem.at[field], recv_sem=recv_sem.at[field],
                device_id=device(xc, yc, z, core), device_id_type=MESH,
            ).start()
        pltpu.make_async_copy(block(src, zc), target, recv_sem.at[field]).start()

    def land(trip):
        dst = buf.at[2 * trip + 1]
        pltpu.make_async_copy(dst, dst, recv_sem.at[trip]).wait()
        return dst

    def landed(trip):
        return land(trip)[...]

    def share(k, value):
        full[k, core] = value
        pltpu.make_async_remote_copy(
            src_ref=full.at[k, core], dst_ref=full.at[k, core],
            send_sem=core_send.at[k], recv_sem=core_recv.at[k],
            device_id=sibling, device_id_type=MESH,
        ).start()

    def shared(k):
        other = full.at[k, 1 - core]
        pltpu.make_async_copy(other, other, core_recv.at[k]).wait()
        return other[...]

    def joined(mine, other):
        first = core == 0
        return jnp.concatenate([jnp.where(first, mine, other), jnp.where(first, other, mine)], axis=1)

    CHEM, RHO, PLUS, TERM, PLUS_BACK, MOVED, MOVED_BACK = range(7)

    loads[0].wait()
    rho = fields[0].T
    buf[2 * RHO] = rho
    loads[1].wait()
    chem = fields[1].T
    buf[2 * CHEM] = chem
    pl.semaphore_wait(barrier, 24)
    for hops in (4, 3, 2, 1):
        tell(ready.at[0], hops)
    for field in (CHEM, RHO):
        across(field)
    loads[2].wait()
    for i in range(6):
        mats[2 * i], mats[2 * i + 1] = split(exact[i])
    pl.semaphore_wait(ready.at[0], 8)
    tell(ready.at[1], 4)
    for field in (CHEM, RHO):
        along(field)
    pl.semaphore_wait(ready.at[1], 2)
    plus = left(hz, chem + step_secrete * rho)
    base[...] = rho - step_chemo * left(dz, rho * left(dz, chem))
    wave = (col * GROUP + zc).astype(jnp.float32)
    wave = jnp.minimum(wave, N - wave)
    loads[3].wait()
    ksquare = marks[...] + wave * wave
    filt[0] = 1.0 / (1.0 + step_motile * ksquare)
    filt[1] = 1.0 / (1.0 + step_diffuse * ksquare + step_decay)

    chem_own = to_plane(landed(CHEM))
    share(0, chem_own)
    slope_x = left(dx, chem_own)
    chem_other = shared(0)
    slope_y = right(joined(chem_own, chem_other), dy)
    rho_own = to_plane(landed(RHO))
    share(1, rho_own)
    term = left(dx, rho_own * slope_x)
    rho_other = shared(1)
    term = term + right_own(joined(rho_own, rho_other) * slope_y, dy)
    leave(TERM, "back", to_plane(term))
    leave(PLUS, "out", plus)

    def solve(which, k, trip):
        mine = to_plane(landed(trip))
        share(k, mine)
        mine = left(hx, mine)
        other = left(hx, shared(k))
        modes = right(joined(mine, other), hy) * filt[which]
        return to_plane(left(hx, right_own(modes, hy)))

    leave(MOVED, "out", left(hz, base[...] - step_chemo * landed(TERM)))
    leave(PLUS_BACK, "back", solve(1, 2, PLUS))
    leave(MOVED_BACK, "back", solve(0, 3, MOVED))

    def store(i, trip):
        final[i] = left(hz, landed(trip)).T
        move = pltpu.make_async_copy(final.at[i], out.at[i], store_sem.at[i])
        move.start()
        return move

    stores = [store(1, PLUS_BACK), store(0, MOVED_BACK)]

    def sent(sem, count):
        rest = buf.at[0, pl.ds(0, count), :]
        pltpu.make_async_copy(rest, rest, sem).wait()

    for field in (CHEM, RHO):
        sent(mid_send.at[field], ROWS - GROUP)
        sent(send_sem.at[field], ROWS - GROUP)
    for trip in (PLUS, TERM, PLUS_BACK, MOVED, MOVED_BACK):
        sent(send_sem.at[trip], ROWS - 1)
    def core_sent(k, carry):
        pltpu.make_async_copy(full.at[0, 0], full.at[0, 0], core_send.at[k]).wait()
        return carry
    lax.fori_loop(0, 4, core_sent, 0)
    for store in stores:
        store.wait()


CHUNK = 64


def finish(both_ref, dens_ref, pher_ref, held, in_sem, out_sem):
    parts = [(i, k) for i in range(2) for k in range(LANES // CHUNK)]

    def load(n, i, k):
        rows = pl.ds(k * CHUNK, CHUNK)
        return pltpu.make_async_copy(both_ref.at[i, rows, :], held.at[i, rows, :], in_sem.at[n])

    def store(n, i, k):
        rows = pl.ds(k * CHUNK, CHUNK)
        target = (dens_ref, pher_ref)[i]
        return pltpu.make_async_copy(held.at[i, rows, :], target.at[rows, :], out_sem.at[n])

    for n, (i, k) in enumerate(parts):
        load(n, i, k).start()
    for n, (i, k) in enumerate(parts):
        load(n, i, k).wait()
        store(n, i, k).start()
    for n, (i, k) in enumerate(parts):
        store(n, i, k).wait()


def per_device(density, pheromone):
    mats, mx, my = tables()
    marks = np.asarray(mx[:, None] + my[None, :], np.float32)
    hbm = pl.BlockSpec(memory_space=pltpu.HBM)
    flat = jax.ShapeDtypeStruct((LANES, N), jnp.float32)
    mats = np.stack(mats)
    both = pl.pallas_call(
        kernel,
        out_shape=jax.ShapeDtypeStruct((2, LANES, N), jnp.float32),
        in_specs=[hbm] * 4,
        out_specs=hbm,
        scratch_shapes=[
            pltpu.VMEM((2, LANES, N), jnp.float32),
            pltpu.VMEM((6, N, N), jnp.float32),
            pltpu.VMEM((12, N, N), jnp.bfloat16),
            pltpu.VMEM((N, N), jnp.float32),
            pltpu.VMEM((14, ROWS, LANES), jnp.float32),
            pltpu.VMEM((2, ROWS, LANES), jnp.float32),
            pltpu.VMEM((2, ROWS, LANES), jnp.float32),
            pltpu.VMEM((2, LANES, N), jnp.float32),
            pltpu.VMEM((4, 2, N, LANES), jnp.float32),
            pltpu.VMEM((ROWS, LANES), jnp.float32),
            pltpu.VMEM((2, N, N), jnp.float32),
            pltpu.SemaphoreType.DMA((4,)),
            pltpu.SemaphoreType.DMA((2,)),
            pltpu.SemaphoreType.DMA((2,)),
            pltpu.SemaphoreType.DMA((2,)),
            pltpu.SemaphoreType.DMA((7,)),
            pltpu.SemaphoreType.DMA((7,)),
            pltpu.SemaphoreType.DMA((4,)),
            pltpu.SemaphoreType.DMA((4,)),
            pltpu.SemaphoreType.REGULAR((2,)),
        ],
        compiler_params=pltpu.CompilerParams(
            collective_id=0, has_side_effects=True, vmem_limit_bytes=60 << 20
        ),
        name="chemotaxis_step",
    )(density.reshape(LANES, N), pheromone.reshape(LANES, N), mats, marks)
    flat = jax.ShapeDtypeStruct((LANES, N), jnp.float32)
    new_d, new_p = pl.pallas_call(
        finish,
        out_shape=(flat, flat),
        in_specs=[hbm],
        out_specs=(hbm, hbm),
        scratch_shapes=[
            pltpu.VMEM((2, LANES, N), jnp.float32),
            pltpu.SemaphoreType.DMA((2 * LANES // CHUNK,)),
            pltpu.SemaphoreType.DMA((2 * LANES // CHUNK,)),
        ],
        compiler_params=pltpu.CompilerParams(vmem_limit_bytes=60 << 20),
        name="outputs",
    )(both)
    return new_d.reshape(density.shape), new_p.reshape(density.shape)


def solution(mesh):
    placed = (P(("gx", "gz"), "gy", None), P(("gx", "gz"), "gy", None))
    return jax.shard_map(
        per_device, mesh=mesh, in_specs=placed, out_specs=placed, check_vma=False
    )
```
